32 devices in a mesh: dp: 16 (over z, y, core), ffn: 2 (over x).
Axes of the slice: x: 2, y: 2, z: 4, core: 2. Of those that a mesh axis runs over, the one named last changes fastest.
Arguments:
- tokens: bfloat16 [256, 208, 768], P(('dp', 'ffn')), may hold values from -6 to 6
- gain_one: float32 [768], replicated, may hold values from 0.25 to 1.75
- shift_one: float32 [768], replicated, may hold values from -2 to 2
- query_weight: bfloat16 [768, 768], replicated, may hold values from -0.21875 to 0.21875
- key_weight: bfloat16 [768, 768], replicated, may hold values from -0.21875 to 0.21875
- value_weight: bfloat16 [768, 768], replicated, may hold values from -0.21875 to 0.21875
- out_weight: bfloat16 [768, 768], replicated, may hold values from -0.875 to 0.875
- gain_two: float32 [768], replicated, may hold values from 0.25 to 1.75
- shift_two: float32 [768], replicated, may hold values from -2 to 2
- up_weight: bfloat16 [768, 3072], P(None, 'ffn'), may hold values from -0.21875 to 0.21875
- down_weight: bfloat16 [3072, 768], P('ffn'), may hold values from -0.109375 to 0.109375
- lengths: int32 [256], P(('dp', 'ffn')), may hold values from 27 to 208, as said below
- projection: float32 [12, 64, 32], replicated, may hold values from -4 to 4
- cotangent: bfloat16 [256, 208, 768], P(('dp', 'ffn')), may hold values from -6 to 6
Outputs:
- mixed: bfloat16 [256, 208, 768], P(('dp', 'ffn'))
- input_grad: bfloat16 [256, 208, 768], P(('dp', 'ffn'))
- gain_one_grad: float32 [768], replicated
- shift_one_grad: float32 [768], replicated
- query_grad: float32 [768, 768], replicated
- key_grad: float32 [768, 768], replicated
- value_grad: float32 [768, 768], replicated
- out_grad: float32 [768, 768], replicated
- gain_two_grad: float32 [768], replicated
- shift_two_grad: float32 [768], replicated
- up_grad: float32 [768, 3072], P(None, 'ffn')
- down_grad: float32 [3072, 768], P('ffn')
The draws below stay inside these ranges and needn't reach their ends.
Inputs may be any that keep to these rules, and one draw needn't show every extreme that they name: `lengths`: each molecule's count of real tokens; its first that many positions are real and the rest padding; some molecule has exactly 208.
All inputs are finite; a program needn't handle non-finite values.
Results may differ from the reference program's by a relative error of at most 0.012.
The reference program's roundings to bfloat16 on the way count: a program that leaves them out, or rounds other values in their place, can miss the bound.
Values may be sent and summed in bfloat16 or wider, within the bound.
A program may use at most 320 MiB of HBM per device.

```python
import jax
import jax.numpy as jnp
from jax import lax

D = 768
H = 12
HD = 64
FF = 3072
FEATURES = 32
SEQ_LEN = 208
MOL_DEV = 8
MOLS = 256


def draw_lengths(key, part):
    key = jax.random.fold_in(key, 11)
    short_key, long_key, pick_key, place_key = jax.random.split(key, 4)
    short_lengths = jax.random.randint(short_key, (MOLS,), SEQ_LEN // 8 + 1, SEQ_LEN // 4 + 1)
    long_lengths = jax.random.randint(long_key, (MOLS,), SEQ_LEN - SEQ_LEN // 16, SEQ_LEN + 1)
    polymer = jax.random.randint(pick_key, (MOLS,), 0, 24) == 0
    chosen = jax.random.randint(place_key, (), 0, MOLS)
    marker = jnp.arange(MOLS) == chosen
    long_lengths = jnp.where(marker, SEQ_LEN, long_lengths)
    polymer = polymer | marker
    return jnp.where(polymer, long_lengths, short_lengths).astype(jnp.int32)


def steps_of(key, extent, shards, least, top_value):
    def one(dim, parts):
        draws = jax.random.uniform(jax.random.fold_in(jax.random.fold_in(key, 6), dim), (parts,), jnp.float32, least / len(shards), top_value / len(shards))
        return jnp.repeat(jnp.exp(draws), extent[dim] // parts).reshape((-1,) + (1,) * (len(extent) - dim - 1))

    loudness = one(*shards[0])
    for cut in shards[1:]:
        loudness = loudness * one(*cut)
    return loudness


def noise(own_key, shape, deviation, reach, cuts=(), held_as=jnp.bfloat16):
    values = deviation * jax.random.normal(own_key, shape, jnp.float32)
    if cuts:
        values = values * steps_of(own_key, shape, cuts, -0.22, 0.18)
    return jnp.clip(values, -reach, reach).astype(held_as)


def setup_inputs(seed: int = 0) -> dict:
    key_list = jax.random.split(jax.random.key(seed), 15)
    tokens = noise(key_list[0], (MOLS, SEQ_LEN, D), 1.0, 6.0, ((0, 32),))
    gain_one = jnp.clip(1.0 + 0.15 * jax.random.normal(key_list[1], (D,), jnp.float32), 0.25, 1.75)
    shift_one = noise(key_list[2], (D,), 0.3, 2.0, (), jnp.float32)
    query_weight = noise(key_list[3], (D, D), D ** -0.5, 0.21875)
    key_weight = noise(key_list[4], (D, D), D ** -0.5, 0.21875)
    value_weight = noise(key_list[5], (D, D), D ** -0.5, 0.21875)
    out_weight = noise(key_list[6], (D, D), (D // 16) ** -0.5, 0.875)
    gain_two = jnp.clip(1.0 + 0.15 * jax.random.normal(key_list[7], (D,), jnp.float32), 0.25, 1.75)
    shift_two = noise(key_list[8], (D,), 0.3, 2.0, (), jnp.float32)
    up_weight = noise(key_list[9], (D, FF), D ** -0.5, 0.21875, ((1, 2),))
    down_weight = noise(key_list[10], (FF, D), FF ** -0.5, 0.109375, ((0, 2),))
    lengths = draw_lengths(jax.random.fold_in(key_list[14], 71), 0)
    projection = noise(key_list[12], (H, HD, FEATURES), 1.0, 4.0, (), jnp.float32)
    cotangent = noise(key_list[13], (MOLS, SEQ_LEN, D), 1.0, 6.0, ((0, 32),))
    return dict(tokens=tokens, gain_one=gain_one, shift_one=shift_one, query_weight=query_weight, key_weight=key_weight, value_weight=value_weight, out_weight=out_weight, gain_two=gain_two, shift_two=shift_two, up_weight=up_weight, down_weight=down_weight, lengths=lengths, projection=projection, cotangent=cotangent)


@jax.custom_vjp
def low(v):
    return lax.optimization_barrier(v.astype(jnp.bfloat16)).astype(jnp.float32)

@jax.custom_vjp
def low_back(v):
    return v

def low_keep(v):
    return (low(v), None)

def low_pass(kept, grad):
    return (grad,)

def back_keep(v):
    return (v, None)

def back_low(kept, grad):
    return (low(grad),)
low.defvjp(low_keep, low_pass)
low_back.defvjp(back_keep, back_low)

def product(left_side, right_side):
    return jnp.dot(left_side, right_side, precision=lax.Precision.HIGHEST, preferred_element_type=jnp.float32)

def layer_norm(values, gain_vector, shift_vector):
    average = lax.optimization_barrier(jnp.mean(values, -1, keepdims=True))
    centered = values - average
    variance = lax.optimization_barrier(jnp.mean(centered * centered, -1, keepdims=True))
    return centered * lax.rsqrt(variance + 1e-05) * gain_vector + shift_vector

def gelu_exact(values):
    return jax.nn.gelu(values, approximate=False)

def rotary_tables(seq_length, head_size):
    half_size = head_size // 2
    frequency = 10000.0 ** (-2.0 * jnp.arange(half_size, dtype=jnp.float32) / head_size)
    angles = jnp.arange(seq_length, dtype=jnp.float32)[:, None] * frequency[None, :]
    return (jnp.cos(angles), jnp.sin(angles))

def rotate(vectors, cosine_table, sine_table):
    half_size = vectors.shape[-1] // 2
    front_half = vectors[..., :half_size]
    back_half = vectors[..., half_size:]
    cosine_table = cosine_table[None, :, None, :]
    sine_table = sine_table[None, :, None, :]
    return jnp.concatenate([front_half * cosine_table - back_half * sine_table, back_half * cosine_table + front_half * sine_table], -1)

def feature_map(vectors, projection):
    scaled = vectors * vectors.shape[-1] ** (-0.25)
    lifted = jnp.einsum('blhd,hdm->blhm', scaled, projection, precision=lax.Precision.HIGHEST)
    return jnp.exp(lifted - 0.5 * lax.optimization_barrier(jnp.sum(scaled * scaled, -1, keepdims=True))) * projection.shape[-1] ** (-0.5)

def linear_attention(queries, keys_proj, values_proj, lengths, projection):
    seq_length = queries.shape[1]
    cosine_table, sine_table = rotary_tables(seq_length, queries.shape[-1])
    queries = rotate(queries, cosine_table, sine_table)
    keys_proj = rotate(keys_proj, cosine_table, sine_table)
    places = jnp.arange(seq_length, dtype=jnp.int32)
    valid_mask = (places[None, :] < lengths[:, None]).astype(queries.dtype)
    query_feat = feature_map(queries, projection)
    key_feat = feature_map(keys_proj, projection) * valid_mask[:, :, None, None]
    kv_state = jnp.einsum('blhm,blhd->bhmd', key_feat, values_proj, precision=lax.Precision.HIGHEST)
    totals = lax.optimization_barrier(jnp.sum(key_feat, axis=1))
    numerator = jnp.einsum('blhm,bhmd->blhd', query_feat, kv_state, precision=lax.Precision.HIGHEST)
    denominator = jnp.einsum('blhm,bhm->blh', query_feat, totals, precision=lax.Precision.HIGHEST) + 1e-06
    return numerator / denominator[..., None]

def block_forward(block_tokens, weights, block_lengths, projection):
    gain_one, shift_one, query_weight, key_weight, value_weight, out_weight, gain_two, shift_two, up_weight, down_weight = weights
    molecules, seq_length, width_model = block_tokens.shape
    token_rows = block_tokens.reshape(molecules * seq_length, width_model)
    normed_one = low(layer_norm(token_rows, gain_one, shift_one))
    queries = low_back(product(normed_one, query_weight)).reshape(molecules, seq_length, H, HD)
    keys_proj = low_back(product(normed_one, key_weight)).reshape(molecules, seq_length, H, HD)
    values_proj = low_back(product(normed_one, value_weight)).reshape(molecules, seq_length, H, HD)
    attended = linear_attention(queries, keys_proj, values_proj, block_lengths, projection)
    attended = low(attended.reshape(molecules * seq_length, width_model))
    branch = low_back(product(attended, out_weight))
    middle = token_rows + branch
    normed_two = low(layer_norm(middle, gain_two, shift_two))
    hidden = low_back(product(normed_two, up_weight))
    activated = low(gelu_exact(hidden))
    return middle + product(activated, down_weight)

def reference(tokens, gain_one, shift_one, query_weight, key_weight, value_weight, out_weight, gain_two, shift_two, up_weight, down_weight, lengths, projection, cotangent):
    weights = (gain_one.astype(jnp.float32), shift_one.astype(jnp.float32), query_weight.astype(jnp.float32), key_weight.astype(jnp.float32), value_weight.astype(jnp.float32), out_weight.astype(jnp.float32), gain_two.astype(jnp.float32), shift_two.astype(jnp.float32), up_weight.astype(jnp.float32), down_weight.astype(jnp.float32))
    projection_f = projection.astype(jnp.float32)
    block_count = MOLS // MOL_DEV
    token_blocks = tokens.reshape(block_count, MOL_DEV, SEQ_LEN, D)
    length_blocks = lengths.reshape(block_count, MOL_DEV)
    cot_blocks = cotangent.reshape(block_count, MOL_DEV, SEQ_LEN, D)

    def block_step(running, pieces):
        block_tokens, block_lengths, block_cot = pieces
        places = jnp.arange(SEQ_LEN, dtype=jnp.int32)
        valid_rows = (places[None, :] < block_lengths[:, None]).astype(jnp.float32)
        masked_cot = block_cot.astype(jnp.float32) * valid_rows[:, :, None]

        def local_forward(block_in, weight_set):
            return block_forward(block_in, weight_set, block_lengths, projection_f)
        result, pullback = jax.vjp(local_forward, block_tokens.astype(jnp.float32), weights)
        grad_in, grad_weights = pullback(masked_cot.reshape(MOL_DEV * SEQ_LEN, D))
        running = jax.tree.map(jnp.add, running, grad_weights)
        return (running, (result.reshape(MOL_DEV, SEQ_LEN, D).astype(jnp.bfloat16), grad_in.reshape(MOL_DEV, SEQ_LEN, D).astype(jnp.bfloat16)))
    zeros_start = jax.tree.map(jnp.zeros_like, weights)
    totals, (outputs, in_grads) = lax.scan(block_step, zeros_start, (token_blocks, length_blocks, cot_blocks))
    mixed = outputs.reshape(MOLS, SEQ_LEN, D)
    input_grad = in_grads.reshape(MOLS, SEQ_LEN, D)
    return (mixed, input_grad, totals[0], totals[1], totals[2], totals[3], totals[4], totals[5], totals[6], totals[7], totals[8], totals[9])
```

```python
import functools
import math

import jax
import jax.numpy as jnp
import numpy as np
from jax import lax
from jax.experimental import pallas as pl
from jax.experimental.pallas import tpu as pltpu
from jax.sharding import PartitionSpec as P

H = 12
HD = 64
BF = jnp.bfloat16
F32 = jnp.float32
GROUP = 4
ROOT = math.sqrt(0.5)
INV_ROOT_TAU = 1.0 / math.sqrt(2.0 * math.pi)
ERFC_P = 0.4
ERFC_C = (0.23131369, 0.16568147, 0.4585619, -0.35877025, 0.70161513, -0.19840191)
SHORT = 64
VMEM_LIMIT = 57 * 1024 * 1024


def nn(a, b):
    return lax.dot_general(a, b, (((1,), (0,)), ((), ())), preferred_element_type=F32)


def nt(a, b):
    return lax.dot_general(a, b, (((1,), (1,)), ((), ())), preferred_element_type=F32)


def tn(a, b):
    return lax.dot_general(a, b, (((0,), (0,)), ((), ())), preferred_element_type=F32)


def split(v):
    high = v.astype(BF)
    return high, (v - high.astype(F32)).astype(BF)


def norm_parts(v):
    mean = jnp.mean(v, -1, keepdims=True)
    centered = v - mean
    scale = lax.rsqrt(jnp.mean(centered * centered, -1, keepdims=True) + 1e-05)
    return centered * scale, scale


def normal_tail(h):
    size = jnp.abs(h)
    under = 1.0 + (ERFC_P * ROOT) * size
    t = pl.reciprocal(under, approx=True)
    t = t * (2.0 - under * t)
    bell = jnp.exp2(h * h * (-0.5 / math.log(2.0)))
    poly = 0.5 * ERFC_C[-1]
    for c in ERFC_C[-2::-1]:
        poly = poly * t + 0.5 * c
    return size, poly * t * bell, bell


def gelu(h):
    size, tail, _ = normal_tail(h)
    return (jnp.maximum(h, 0.0) - size * tail).astype(BF)


def gelu_slope(h):
    size, tail, bell = normal_tail(h)
    act = jnp.maximum(h, 0.0) - size * tail
    return act.astype(BF), jnp.where(h < 0, tail, 1.0 - tail) + h * bell * INV_ROOT_TAU


def rotate(u, cos, sin):
    out = []
    first = lax.broadcasted_iota(jnp.int32, (u.shape[0], 128), 1) % 64 < 32
    for k in range(u.shape[1] // 128):
        part = u[:, 128 * k : 128 * (k + 1)]
        other = jnp.where(first, pltpu.roll(part, 96, 1), pltpu.roll(part, 32, 1))
        out.append(part * cos + other * sin)
    return jnp.concatenate(out, 1)


def rotary_tables(length):
    half = HD // 2
    freq = (10000.0 ** (-2.0 * np.arange(half, dtype=np.float32) / HD)).astype(np.float32)
    angles = np.arange(length, dtype=np.float32)[:, None] * freq[None, :]
    cos = np.cos(angles.astype(np.float64)).astype(np.float32)
    sin = np.sin(angles.astype(np.float64)).astype(np.float32)
    return np.tile(cos, (1, 4)), np.concatenate([-sin, sin, -sin, sin], 1)


def head_mask(features):
    row = np.arange(GROUP * features)[:, None] // features
    lane = np.arange(GROUP * HD)[None, :] // HD
    return (row == lane).astype(np.float32)


def build_features(projection, forward, back):
    heads, features, size = projection.shape
    wide, deep = GROUP * size, GROUP * features
    spread = (
        lax.broadcasted_iota(jnp.int32, (size, wide), 1) % size
        == lax.broadcasted_iota(jnp.int32, (size, wide), 0)
    ).astype(F32).astype(BF)
    inside = (
        lax.broadcasted_iota(jnp.int32, (deep, wide), 0) // features
        == lax.broadcasted_iota(jnp.int32, (deep, wide), 1) // size
    )
    norm = jnp.where(inside, -1.0 / 16.0, 0.0)
    one = jnp.where(inside, 1.0 / 8.0, 0.0).astype(BF)
    for g in range(heads // GROUP):
        block = projection[g * GROUP : (g + 1) * GROUP].reshape(deep, size) * size ** (-0.25)
        high, low = (jnp.where(inside, nn(piece, spread), 0.0) for piece in split(block))
        if forward is not None:
            for i, piece in enumerate((high, high, low, norm, norm)):
                forward[g, wide * i : wide * (i + 1), :] = piece.T.astype(BF)
        if back is not None:
            for i, (piece, other) in enumerate(((high, one), (high, one), (low, jnp.zeros_like(one)))):
                back[g, deep * i : deep * (i + 1), :wide] = piece.astype(BF)
                back[g, deep * i : deep * (i + 1), wide:] = other


def line(ref):
    return ref[...].reshape(1, ref.shape[0])


def features_of(u, weights, features):
    high, low = split(u)
    square_high, square_low = split(u * u)
    lhs = jnp.concatenate([high, low, high, square_high, square_low], 1)
    return jnp.exp(nn(lhs, weights)) * features ** (-0.5)


def with_ones(values):
    values = values.astype(BF)
    return jnp.concatenate([values, jnp.ones_like(values)], 1)


def stacked(state):
    return jnp.concatenate(split(state), 0)


def times_state(left, state):
    return nn(jnp.concatenate([left, left], 1), state)


def times_state_back(pair, state):
    rows, count = pair[0].shape[0], state.shape[0] // 2
    out = nt(jnp.concatenate(pair, 0), state)
    return out[:rows, :count] + out[:rows, count:] + out[rows:, :count]


def attend(items, mask):
    states = [stacked(tn(phi_k, values) * mask) for _, phi_k, values in items]
    boths = [times_state(phi_q, state) for (phi_q, _, _), state in zip(items, states)]
    out = []
    for both, state in zip(boths, states):
        lanes = both.shape[1] // 2
        sums = both[:, lanes:] + 1e-06
        under = pl.reciprocal(sums, approx=True)
        under = under * (2.0 - sums * under)
        out.append((both[:, :lanes] * under, under, state))
    return out


def attend_back(items, results, overs, mask):
    pulls = []
    for (attended, _, _), over in zip(results, overs):
        pulls.append(split(jnp.concatenate([over, -over * attended], 1)))
    dstates = [
        tn(jnp.concatenate([phi_q, phi_q], 0), jnp.concatenate(pull, 0)) * mask
        for (phi_q, _, _), pull in zip(items, pulls)
    ]
    dphi_q = [times_state_back(pull, state) for pull, (_, _, state) in zip(pulls, results)]
    dstates = [stacked(dstate) for dstate in dstates]
    dphi_k = [nt(values, dstate) for (_, _, values), dstate in zip(items, dstates)]
    lanes = overs[0].shape[1]
    dv = [times_state(phi_k, dstate[:, :lanes]) for (_, phi_k, _), dstate in zip(items, dstates)]
    half = dphi_k[0].shape[1] // 2
    return [(a, b[:, :half] + b[:, half:], c) for a, b, c in zip(dphi_q, dphi_k, dv)]


def pull_features(dlog, u, back):
    high, low = split(dlog)
    out = nn(jnp.concatenate([high, low, high], 1), back)
    lanes = u.shape[1]
    return out[:, :lanes] - u * out[:, lanes:]


MESH = pl.DeviceIdType.MESH


class Place:
    def __init__(self, stages):
        dp, ffn = lax.axis_index("dp"), lax.axis_index("ffn")
        self.bits, self.partners = {}, {}
        for stage in stages:
            if stage == "ffn":
                self.bits[stage], self.partners[stage] = ffn, {"ffn": 1 - ffn}
            else:
                bit = dp // (1 << stage) % 2
                self.bits[stage], self.partners[stage] = bit, {"dp": dp + (1 - 2 * bit) * (1 << stage)}


class Gather:
    STAGES = ("ffn", 1, 2, 0)
    SHARES = (2, 2, 1, 1)
    COPIES = 8

    def __init__(self, sources, targets, sends, recvs):
        self.place = Place(self.STAGES)
        self.sources, self.targets, self.sends, self.recvs = sources, targets, sends, recvs

    def copy(self, array, lane, kind, part=0):
        source, target = self.sources[array], self.targets[array]
        axes = (1, 2) if lane % 2 == 0 else (2, 1)
        bits = dict(self.place.bits)
        for index, axis in enumerate(axes):
            if part >> index & 1:
                bits[axis] = 1 - bits[axis]
        eighth = source.shape[0] // 8
        unit = eighth // sum(self.SHARES)
        size = unit * self.SHARES[lane]
        first = (4 * bits[1] + 2 * bits[2] + bits[0]) * eighth + unit * sum(self.SHARES[:lane])
        rows = pl.ds(pl.multiple_of(first, 16), size)
        stage = {"ffn": "ffn", "first": axes[0], "second": axes[1], "core": 0}[kind]
        index = {"ffn": 0, "first": 1, "second": 2, "core": 4}[kind] + part
        return pltpu.make_async_remote_copy(
            src_ref=(source if kind == "ffn" else target).at[rows, :],
            dst_ref=target.at[rows, :],
            send_sem=self.sends.at[array, lane, index],
            recv_sem=self.recvs.at[array, lane, index],
            device_id=self.place.partners[stage],
            device_id_type=MESH,
        )

    def begin(self):
        sem = pltpu.get_barrier_semaphore()
        for stage in self.STAGES:
            pl.semaphore_signal(sem, inc=1, device_id=self.place.partners[stage], device_id_type=MESH)
        pl.semaphore_wait(sem, len(self.STAGES))
        for lane in range(2):
            for array in range(2):
                self.copy(array, lane, "ffn").start()

    def arrive(self, lane, kind, part=0):
        for array in range(2):
            self.copy(array, lane, kind, part).wait_recv()
            if kind == "ffn":
                if lane + 2 < len(self.SHARES):
                    self.copy(array, lane + 2, "ffn").start()
                self.copy(array, lane, "first").start()
                self.copy(array, lane, "second").start()
                self.copy(array, lane, "core").start()
            elif kind == "first":
                self.copy(array, lane, "second", 1).start()
                self.copy(array, lane, "core", 1).start()
            else:
                self.copy(array, lane, "core", 2 + part).start()

    def end(self):
        lanes = range(len(self.SHARES))
        for lane in lanes:
            for array in range(2):
                for part in range(4):
                    self.copy(array, lane, "core", part).wait_recv()
        for lane in lanes:
            for array in range(2):
                for kind, parts in (("ffn", 1), ("first", 1), ("second", 2), ("core", 4)):
                    for part in range(parts):
                        self.copy(array, lane, kind, part).wait_send()


ARRIVALS = (
    ("ffn", 0, (1, 2, 3, 4)), ("first", 0, (4, 4, 6, 7)), ("second", 0, (4, 5, 6, 7)), ("second", 1, (8, 8, 9, 9)),
)


def row_strips(rows, most=64):
    return [(start, min(most, rows - start)) for start in range(0, rows, most)]


def attention_forward_kernel(
    per, steps, lengths, x_ref, g1, s1, wq, wk, wv, wo, g2, s2, cos_ref, sin_ref, proj_ref, mask_ref, up_hbm, down_hbm,
    middle_ref, normed_ref, up_other, down_other, u_out, v_out, phi_out, att_out, under_out, low_out, state_out,
    q_s, k_s, v_s, a_s, low_s, fw_s, sends, recvs,
):
    step = pl.program_id(0)
    seq = x_ref.shape[1]
    width = x_ref.shape[2]
    features = proj_ref.shape[1]
    gather = Gather((up_hbm, down_hbm), (up_other, down_other), sends, recvs)

    @pl.when(step == 0)
    def _():
        gather.begin()
        build_features(proj_ref, fw_s, None)

    strips = [(m, start, count) for m in range(per) for start, count in row_strips(seq)]
    gain, shift = line(g1), line(s1)
    for m, start, count in strips:
        n, _ = norm_parts(x_ref[m, start : start + count, :].astype(F32))
        low_s[m * seq + start : m * seq + start + count, :] = (n * gain + shift).astype(BF)
    low = low_s[...]
    low_out[...] = low.reshape(per, seq, width)[:, :SHORT, :]
    q_s[...] = nn(low, wq[...])
    k_s[...] = nn(low, wk[...])
    v_s[...] = nn(low, wv[...])
    cos, sin = cos_ref[...], sin_ref[...]
    lanes = GROUP * HD
    mask = mask_ref[...]
    slots = 3 * steps

    def pass_on(place):
        for at in range(place, slots, 3):
            due = [
                (lane, kind, part)
                for kind, part, places in ARRIVALS
                for lane, twelfth in enumerate(places)
                if twelfth * slots // 12 == at
            ]
            if due:

                @pl.when(step == at // 3)
                def _(due=due):
                    for lane, kind, part in due:
                        gather.arrive(lane, kind, part)

    pass_on(0)
    deep = GROUP * features
    blocks = [
        (m, g, slice(m * seq, (m + 1) * seq), slice(g * lanes, (g + 1) * lanes))
        for m in range(per)
        for g in range(H // GROUP)
    ]
    valid = [
        (lax.broadcasted_iota(jnp.int32, (seq, deep), 0) < lengths[step * per + m]).astype(F32) for m in range(per)
    ]
    turned = [
        jnp.concatenate([rotate(q_s[rows, cols], cos, sin), rotate(k_s[rows, cols], cos, sin)], 0)
        for _, _, rows, cols in blocks
    ]
    phis = [features_of(u, fw_s[g], features) for (_, g, _, _), u in zip(blocks, turned)]
    phis = [(phi[:seq], phi[seq:] * valid[m]) for (m, _, _, _), phi in zip(blocks, phis)]
    items = [
        (phi_q.astype(BF), phi_k.astype(BF), with_ones(v_s[rows, cols]))
        for (phi_q, phi_k), (_, _, rows, cols) in zip(phis, blocks)
    ]
    results = attend(items, mask)
    for (m, g, rows, cols), u, phi, (attended, under, state) in zip(blocks, turned, phis, results):
        a_s[rows, cols] = attended.astype(BF)
        u_out[0, m, :, cols] = u[:SHORT]
        u_out[1, m, :, cols] = u[seq : seq + SHORT]
        v_out[m, :, cols] = v_s[m * seq : m * seq + SHORT, cols].astype(BF)
        for j in range(2):
            phi_out[j, m, :, g * deep : (g + 1) * deep] = phi[j][:SHORT]
        att_out[m, :, cols] = attended[:SHORT]
        under_out[m, :, cols] = under[:SHORT]
        state_out[m, g] = state
    pass_on(1)
    middle_ref[...] = nn(a_s[...], wo[...])
    gain, shift = line(g2), line(s2)
    for m, start, count in strips:
        rows = slice(m * seq + start, m * seq + start + count)
        middle = x_ref[m, start : start + count, :].astype(F32) + middle_ref[rows, :]
        middle_ref[rows, :] = middle
        n, _ = norm_parts(middle)
        normed_ref[rows, :] = (n * gain + shift).astype(BF)
    pass_on(2)

    @pl.when(step == steps - 1)
    def _():
        gather.end()


def full(shape, **kw):
    return pl.BlockSpec(shape, lambda i, *_: (0,) * len(shape), **kw)


def attention_forward(tokens, lengths, g1, s1, wq, wk, wv, wo, g2, s2, tables, projection, mask, up, down, per=2):
    mols, seq, width = tokens.shape
    rows = per * seq
    cos, sin = tables
    heads, features, size = projection.shape
    states = (heads // GROUP, 2 * GROUP * features, 2 * GROUP * size)
    one = full((width,))
    square = full((width, width))
    hbm = pl.BlockSpec(memory_space=pl.ANY)
    return pl.pallas_call(
        functools.partial(attention_forward_kernel, per, mols // per),
        grid=(mols // per,),
        in_specs=[
            pl.BlockSpec(memory_space=pltpu.SMEM),
            pl.BlockSpec((per, seq, width), lambda i: (i, 0, 0)),
            one, one, square, square, square, square, one, one,
            full(cos.shape), full(sin.shape), full(projection.shape), full(mask.shape), hbm, hbm,
        ],
        out_specs=[
            pl.BlockSpec((rows, width), lambda i: (i, 0)),
            pl.BlockSpec((rows, width), lambda i: (i, 0)),
            hbm, hbm,
            pl.BlockSpec((2, per, SHORT, width), lambda i: (0, i, 0, 0)),
            pl.BlockSpec((per, SHORT, width), lambda i: (i, 0, 0)),
            pl.BlockSpec((2, per, SHORT, heads * features), lambda i: (0, i, 0, 0)),
            pl.BlockSpec((per, SHORT, width), lambda i: (i, 0, 0)),
            pl.BlockSpec((per, SHORT, width), lambda i: (i, 0, 0)),
            pl.BlockSpec((per, SHORT, width), lambda i: (i, 0, 0)),
            pl.BlockSpec((per,) + states, lambda i: (i, 0, 0, 0)),
        ],
        scratch_shapes=[pltpu.VMEM((rows, width), F32)] * 3
        + [
            pltpu.VMEM((rows, width), BF),
            pltpu.VMEM((rows, width), BF),
            pltpu.VMEM((heads // GROUP, 5 * GROUP * size, GROUP * features), BF),
            pltpu.SemaphoreType.DMA((2, len(Gather.SHARES), Gather.COPIES)),
            pltpu.SemaphoreType.DMA((2, len(Gather.SHARES), Gather.COPIES)),
        ],
        out_shape=[
            jax.ShapeDtypeStruct((mols * seq, width), F32),
            jax.ShapeDtypeStruct((mols * seq, width), BF),
            jax.ShapeDtypeStruct(up.shape, BF),
            jax.ShapeDtypeStruct(down.shape, BF),
            jax.ShapeDtypeStruct((2, mols, SHORT, width), F32),
            jax.ShapeDtypeStruct((mols, SHORT, width), BF),
            jax.ShapeDtypeStruct((2, mols, SHORT, heads * features), F32),
            jax.ShapeDtypeStruct((mols, SHORT, width), F32),
            jax.ShapeDtypeStruct((mols, SHORT, width), F32),
            jax.ShapeDtypeStruct((mols, SHORT, width), BF),
            jax.ShapeDtypeStruct((mols,) + states, BF),
        ],
        compiler_params=pltpu.CompilerParams(
            vmem_limit_bytes=VMEM_LIMIT, collective_id=1, has_side_effects=True
        ),
        name="attention_forward",
    )(lengths, tokens, g1, s1, wq, wk, wv, wo, g2, s2, cos, sin, projection, mask, up, down)


def offsets_of(lengths, starts, counts):
    def one(b, total):
        count = (lengths[b] + 15) // 16
        starts[b] = total
        counts[b] = count
        return total + count

    return lax.fori_loop(0, lengths.shape[0], one, jnp.int32(0))


def pack(source, target, sem, starts, counts, seq, wait):
    def molecule(b, carry):
        origin = b * seq

        def one(i, inner):
            copy = pltpu.make_async_copy(
                source.at[pl.ds(pl.multiple_of(origin + i * 16, 16), 16), :],
                target.at[pl.ds(pl.multiple_of((starts[b] + i) * 16, 16), 16), :],
                sem,
            )
            if wait:
                copy.wait()
            else:
                copy.start()
            return inner

        return lax.fori_loop(0, counts[b], one, carry)

    lax.fori_loop(0, starts.shape[0], molecule, 0)


TILE = 256
FF_CHUNK = 256


def by_rows(count, step, run):
    def one(i, carry):
        run(pl.ds(pl.multiple_of(i * step, 16), step))
        return carry

    lax.fori_loop(0, count // step, one, 0)


def ffn_backward_kernel(
    seq, lengths, normed_hbm, cot_hbm, middle_hbm, up_a, up_b, down_a, down_b, g2,
    grad_ref, mg_ref, slots_hbm, norm_ref, n_s, c_s, ups, downs, u_acc, d_acc, back_s, starts, counts, sems, slot_sems,
):
    mols = lengths.shape[0]
    total = offsets_of(lengths, starts, counts)
    width, half = ups.shape[1:]
    moves = ((normed_hbm, n_s, sems.at[0]), (cot_hbm, c_s, sems.at[1]), (middle_hbm, mg_ref, sems.at[2]))
    for source, target, sem in moves:
        pack(source, target, sem, starts, counts, seq, False)
    loads = [
        pltpu.make_async_copy(source, target, sems.at[3 + i])
        for i, (source, target) in enumerate(
            ((up_a, ups.at[0]), (down_a, downs.at[0]), (up_b, ups.at[1]), (down_b, downs.at[1]))
        )
    ]
    for copy in loads:
        copy.start()

    def zero(rows):
        for part in range(2):
            u_acc[part, rows, :] = jnp.zeros((rows.size, half), F32)

    def zero_tall(rows):
        for part in range(2):
            d_acc[part, rows, :] = jnp.zeros((rows.size, width), F32)

    by_rows(width, 32, zero)
    by_rows(half, 64, zero_tall)
    norm_ref[...] = jnp.zeros_like(norm_ref)
    for source, target, sem in moves:
        pack(source, target, sem, starts, counts, seq, True)

    def clear(b, carry):
        last = pl.multiple_of((starts[b] + counts[b] - 1) * 16, 16)
        place = lax.broadcasted_iota(jnp.int32, (16, width), 0) + (counts[b] - 1) * 16
        c_s[pl.ds(last, 16), :] = jnp.where(place < lengths[b], c_s[pl.ds(last, 16), :].astype(F32), 0.0).astype(BF)
        return carry

    lax.fori_loop(0, mols, clear, 0)
    end = total * 16

    def blank(i, carry):
        rows = pl.ds(pl.multiple_of(end + i * 16, 16), 16)
        for ref in (n_s, c_s, mg_ref):
            ref[rows, :] = jnp.zeros((16, width), ref.dtype)
        return carry

    lax.fori_loop(0, TILE // 16, blank, 0)
    for copy in loads:
        copy.wait()
    chunks = [(part, j) for part in range(2) for j in range(half // FF_CHUNK)]

    def tile(start, count):
        rows = pl.ds(pl.multiple_of(start, 128), count)
        n = n_s[rows, :]
        c = c_s[rows, :]

        def enter(part, j):
            cols = slice(j * FF_CHUNK, (j + 1) * FF_CHUNK)
            return nn(n, ups[part, :, cols]), nt(c, downs[part, cols, :])

        ahead = enter(*chunks[0])
        for at, (part, j) in enumerate(chunks):
            cols = slice(j * FF_CHUNK, (j + 1) * FF_CHUNK)
            h, grad = ahead
            if at + 1 < len(chunks):
                ahead = enter(*chunks[at + 1])
            act, slope = gelu_slope(h)
            hg = (grad * slope).astype(BF)
            back = nt(hg, ups[part, :, cols])
            if at == 0:
                back_s[:count, :] = back
            else:
                back_s[:count, :] += back
            d_acc[part, cols, :] += tn(act, c)
            u_acc[part, :, cols] += tn(n, hg)
        back = back_s[:count, :]
        normal, scale = norm_parts(mg_ref[rows, :])
        e = back * line(g2)
        mean_e = jnp.mean(e, -1, keepdims=True)
        mean_en = jnp.mean(e * normal, -1, keepdims=True)
        mg_ref[rows, :] = c.astype(F32) + scale * (e - mean_e - normal * mean_en)
        norm_ref[0:1, :] += jnp.sum(back * normal, 0, keepdims=True)
        norm_ref[1:2, :] += jnp.sum(back, 0, keepdims=True)

    def whole_tile(i, carry):
        tile(i * TILE, TILE)
        return carry

    whole = (end + TILE // 2 - 1) // TILE
    lax.fori_loop(0, whole, whole_tile, 0)
    pl.when(whole * TILE < end)(lambda: tile(whole * TILE, TILE // 2))

    slots = [
        pltpu.make_async_copy(
            mg_ref.at[pl.ds(pl.multiple_of(starts[b] * 16, 16), SHORT), :],
            slots_hbm.at[pl.ds(b * SHORT, SHORT), :],
            slot_sems.at[b],
        )
        for b in range(mols)
    ]
    for copy in slots:
        copy.start()
    copies = []
    for part in range(2):

        def narrow(rows, part=part):
            ups[part, rows, :] = u_acc[part, rows, :].astype(BF)

        def narrow_tall(rows, part=part):
            downs[part, rows, :] = d_acc[part, rows, :].astype(BF)

        by_rows(width, 32, narrow)
        by_rows(half, 64, narrow_tall)
        first = len(copies)
        for j in range(half // 256):
            copies.append((ups.at[part, :, pl.ds(256 * j, 256)], part, j * width, width))
        for j in range(width // 256):
            copies.append((downs.at[part, :, pl.ds(256 * j, 256)], part, half // 256 * width + j * half, half))
        for k in range(first, len(copies)):
            source, _, base, count = copies[k]
            copies[k] = pltpu.make_async_copy(source, grad_ref.at[part, pl.ds(base, count), :], sems.at[7 + k])
            copies[k].start()
    for copy in copies + slots:
        copy.wait()


def ffn_backward(normed, cot, middle, up_a, up_b, down_a, down_b, g2, lengths, seq):
    rows, width = normed.shape
    half = up_a.shape[1]
    hbm = pl.BlockSpec(memory_space=pl.ANY)
    vmem = pl.BlockSpec(memory_space=pltpu.VMEM)
    block_rows = half // 256 * width + width // 256 * half
    return pl.pallas_call(
        functools.partial(ffn_backward_kernel, seq),
        in_specs=[pl.BlockSpec(memory_space=pltpu.SMEM)] + [hbm] * 7 + [vmem],
        out_specs=[hbm, vmem, hbm, vmem],
        out_shape=[
            jax.ShapeDtypeStruct((2, block_rows, 256), BF),
            jax.ShapeDtypeStruct((rows + TILE, width), F32),
            jax.ShapeDtypeStruct((lengths.shape[0] * SHORT, width), F32),
            jax.ShapeDtypeStruct((8, width), F32),
        ],
        scratch_shapes=[
            pltpu.VMEM((rows + TILE, width), BF),
            pltpu.VMEM((rows + TILE, width), BF),
            pltpu.VMEM((2, width, half), BF),
            pltpu.VMEM((2, half, width), BF),
            pltpu.VMEM((2, width, half), F32),
            pltpu.VMEM((2, half, width), F32),
            pltpu.VMEM((TILE, width), F32),
            pltpu.SMEM(lengths.shape, jnp.int32),
            pltpu.SMEM(lengths.shape, jnp.int32),
            pltpu.SemaphoreType.DMA((7 + 2 * (half // 256 + width // 256),)),
            pltpu.SemaphoreType.DMA(lengths.shape),
        ],
        compiler_params=pltpu.CompilerParams(vmem_limit_bytes=VMEM_LIMIT),
        name="ffn_backward",
    )(lengths, normed, cot, middle, up_a, up_b, down_a, down_b, g2)


def long_backward_kernel(
    lengths, x_hbm, mg_hbm, g1, s1, wq_h, wk_h, wv_h, wo_h, cos_ref, sin_ref, proj_ref, mask_ref,
    ig_ref, grad_ref, norm_ref, x_s, mg_s, acc, out_s, fw_s, bw_s, wq, wk, wv, wo, starts, counts, sems, row_sems,
):
    mols, seq, width = x_s.shape
    features = proj_ref.shape[1]
    blocks = width // 256
    lanes = GROUP * HD
    offsets_of(lengths, starts, counts)
    some = lax.fori_loop(0, mols, lambda b, most: jnp.maximum(most, lengths[b]), jnp.int32(0)) > SHORT
    loads = [
        pltpu.make_async_copy(source, target, sems.at[i])
        for i, (source, target) in enumerate(((wq_h, wq), (wk_h, wk), (wv_h, wv), (wo_h, wo)))
    ]

    def row_loads(b):
        return (
            pltpu.make_async_copy(x_hbm.at[b], x_s.at[b], row_sems.at[0, b]),
            pltpu.make_async_copy(
                mg_hbm.at[pl.ds(pl.multiple_of(starts[b] * 16, 16), seq), :], mg_s.at[b], row_sems.at[1, b]
            ),
        )

    def begin(b, carry):
        @pl.when(lengths[b] > SHORT)
        def _():
            for copy in row_loads(b):
                copy.start()

        return carry

    @pl.when(some)
    def _():
        for copy in loads:
            copy.start()
        lax.fori_loop(0, mols, begin, 0)

    norm_ref[...] = jnp.zeros_like(norm_ref)

    def clear(b, carry):
        ig_ref[b] = jnp.zeros((seq, width), BF)
        return carry

    lax.fori_loop(0, mols, clear, 0)

    @pl.when(some)
    def _():
        build_features(proj_ref, fw_s, bw_s)

        def clear_sums(rows):
            acc[rows, :] = jnp.zeros((rows.size, width), F32)

        by_rows(4 * width, 96, clear_sums)
        for copy in loads:
            copy.wait()

    def molecule(b):
        for copy in row_loads(b):
            copy.wait()
        gain = line(g1)
        normal, scale = norm_parts(x_s[b].astype(F32))
        low = (normal * gain + line(s1)).astype(BF)
        inside = lax.broadcasted_iota(jnp.int32, (seq, width), 0) < lengths[b]
        middle_grad = jnp.where(inside, mg_s[b], 0.0)
        branch = middle_grad.astype(BF)
        q, k, v = (nn(low, w[...]) for w in (wq, wk, wv))
        grad = nt(branch, wo[...])
        cos, sin = cos_ref[...], sin_ref[...]
        mask = mask_ref[...]
        cuts = [slice(g * lanes, (g + 1) * lanes) for g in range(H // GROUP)]
        turned = [jnp.concatenate([rotate(q[:, cut], cos, sin), rotate(k[:, cut], cos, sin)], 0) for cut in cuts]
        phis = [features_of(u, fw_s[g], features) for g, u in enumerate(turned)]
        phis = [(phi[:seq], jnp.where(inside[:, : phi.shape[1]], phi[seq:], 0.0)) for phi in phis]
        items = [
            (phi_q.astype(BF), phi_k.astype(BF), with_ones(v[:, cut])) for (phi_q, phi_k), cut in zip(phis, cuts)
        ]
        results = attend(items, mask)
        attended = jnp.concatenate([result[0].astype(BF) for result in results], 1)
        backs = attend_back(items, results, [grad[:, cut] * result[1] for cut, result in zip(cuts, results)], mask)
        dus = [
            pull_features(jnp.concatenate([dphi_q * phi_q, dphi_k * phi_k], 0), u, bw_s[g])
            for g, ((dphi_q, dphi_k, _), (phi_q, phi_k), u) in enumerate(zip(backs, phis, turned))
        ]
        dq = jnp.concatenate([rotate(du[:seq], cos, -sin).astype(BF) for du in dus], 1)
        dk = jnp.concatenate([rotate(du[seq:], cos, -sin).astype(BF) for du in dus], 1)
        dv = jnp.concatenate([back[2].astype(BF) for back in backs], 1)
        for part, (left, right) in enumerate(((attended, branch), (low, dv), (low, dq), (low, dk))):
            acc[part * width : (part + 1) * width, :] += tn(left, right)
        normed_grad = nt(dq, wq[...]) + nt(dk, wk[...]) + nt(dv, wv[...])
        e = normed_grad * gain
        mean_e = jnp.mean(e, -1, keepdims=True)
        mean_en = jnp.mean(e * normal, -1, keepdims=True)
        ig_ref[b] = (middle_grad + scale * (e - mean_e - normal * mean_en)).astype(BF)
        norm_ref[0:1, :] += jnp.sum(normed_grad * normal, 0, keepdims=True)
        norm_ref[1:2, :] += jnp.sum(normed_grad, 0, keepdims=True)

    def each(b, carry):
        pl.when(lengths[b] > SHORT)(functools.partial(molecule, b))
        return carry

    lax.fori_loop(0, mols, each, 0)

    def put(i):
        part, j = i // blocks, i % blocks
        return pltpu.make_async_copy(
            out_s.at[pl.ds(part * width, width), pl.ds(256 * j, 256)], grad_ref.at[pl.ds(i * width, width), :], sems.at[4 + i]
        )

    @pl.when(some)
    def _():
        for part in range(4):

            def narrow(rows, part=part):
                rows = pl.ds(pl.multiple_of(part * width + rows.start, 16), rows.size)
                out_s[rows, :] = acc[rows, :].astype(BF)

            by_rows(width, 96, narrow)
            for j in range(blocks):
                put(part * blocks + j).start()
        for i in range(4 * blocks):
            put(i).wait()

    @pl.when(jnp.logical_not(some))
    def _():
        def clear_out(rows):
            out_s[rows, :] = jnp.zeros((rows.size, width), BF)

        by_rows(width, 96, clear_out)
        copies = [
            pltpu.make_async_copy(
                out_s.at[pl.ds(0, width), pl.ds(0, 256)], grad_ref.at[pl.ds(i * width, width), :], sems.at[4 + i]
            )
            for i in range(4 * blocks)
        ]
        for copy in copies:
            copy.start()
        for copy in copies:
            copy.wait()


def long_backward(tokens, mg, lengths, g1, s1, wq, wk, wv, wo, tables, projection, mask):
    mols, seq, width = tokens.shape
    heads, features, size = projection.shape
    cos, sin = tables
    hbm = pl.BlockSpec(memory_space=pl.ANY)
    vmem = pl.BlockSpec(memory_space=pltpu.VMEM)
    return pl.pallas_call(
        long_backward_kernel,
        in_specs=[pl.BlockSpec(memory_space=pltpu.SMEM)] + [hbm] * 2 + [vmem] * 2 + [hbm] * 4 + [vmem] * 4,
        out_specs=[vmem, hbm, vmem],
        out_shape=[
            jax.ShapeDtypeStruct((mols, seq, width), BF),
            jax.ShapeDtypeStruct((4 * (width // 256) * width, 256), BF),
            jax.ShapeDtypeStruct((8, width), F32),
        ],
        scratch_shapes=[
            pltpu.VMEM((mols, seq, width), BF),
            pltpu.VMEM((mols, seq, width), F32),
            pltpu.VMEM((4 * width, width), F32),
            pltpu.VMEM((4 * width, width), BF),
            pltpu.VMEM((heads // GROUP, 5 * GROUP * size, GROUP * features), BF),
            pltpu.VMEM((heads // GROUP, 3 * GROUP * features, 2 * GROUP * size), BF),
        ]
        + [pltpu.VMEM((width, width), BF)] * 4
        + [
            pltpu.SMEM(lengths.shape, jnp.int32),
            pltpu.SMEM(lengths.shape, jnp.int32),
            pltpu.SemaphoreType.DMA((4 + 4 * (width // 256),)),
            pltpu.SemaphoreType.DMA((2, mols)),
        ],
        compiler_params=pltpu.CompilerParams(vmem_limit_bytes=VMEM_LIMIT),
        name="long_backward",
    )(lengths, tokens, mg, g1, s1, wq, wk, wv, wo, cos, sin, projection, mask)


def link_of(stage):
    return stage if stage in ("ffn", 0, 1) else 2


class Piece:
    def __init__(self, kind, index, rows, order):
        self.kind, self.first, self.rows = kind, index * rows, rows
        size, slabs = rows, 2 if kind == "F" else 1
        self.reduce, self.gather, self.slabs = [], [], []
        for stage in order:
            if kind == "F" and stage == "ffn":
                slabs = 1
                self.reduce.append((stage, size, "slab"))
            elif size % 32:
                self.reduce.append((stage, size, "whole"))
            else:
                size //= 2
                self.reduce.append((stage, size, "half"))
                self.gather.append((stage, size))
            self.slabs.append(slabs)
        self.size = size
        self.gather.reverse()
        self.steps = len(self.reduce) + len(self.gather)

    def traffic(self, step):
        n = len(self.reduce)
        stage, size = self.reduce[step][:2] if step < n else self.gather[step - n]
        return stage, size * 512 * (self.slabs[step] if step < n else 1)


class Norms:
    kind = "N"

    def __init__(self, order):
        self.order = order
        self.steps = len(order)

    def traffic(self, step):
        return self.order[step], 25000


def pieces_of(dp, block_rows, att_rows):
    tail = list(range(1, dp.bit_length() - 1))
    near, far, rest = tail[:1], tail[1:2], tail[2:]
    cut = lambda rows, shards, choices: next(p for p in choices if rows % (p * shards * 16) == 0 or p == 1)
    pf, pa = cut(block_rows, dp, (4, 3, 2, 1)), cut(att_rows, 2 * dp, (6, 3, 2, 1))
    f_orders = [near + far + ["ffn"] + rest, far + near + ["ffn"] + rest] + [tail + ["ffn"]] * 2
    a_orders = [near + ["ffn"] + far + rest, ["ffn"] + tail]
    f = [Piece("F", i, block_rows // pf, [0] + f_orders[i]) for i in range(pf)]
    a = [Piece("A", i, att_rows // pa, [0] + a_orders[i % 2]) for i in range(pa)]
    return f, a, Norms([0, "ffn"] + tail)


def schedule(pieces, ready, units):
    rate = {0: 300e3, 1: 43e3, 2: 43e3, "ffn": 43e3}
    free, flying, events = {}, [], []

    def start(now, piece, step):
        stage, size = piece.traffic(step)
        link = link_of(stage)
        cost = size / rate[link] * (2 if stage not in ("ffn", 0, 1, 2) else 1)
        free[link] = max(free.get(link, 0.0), now) + cost
        flying.append((free[link] + 2.5, len(events), piece, step))

    now, unit = 3.0, 0
    waiting = list(pieces)
    while flying or waiting or unit < len(units):
        for piece in [p for p in waiting if ready[p] <= unit]:
            if sum(f[3] == 0 and f[2].kind == piece.kind for f in flying) < 2:
                waiting.remove(piece)
                events.append((unit, piece, -1))
                start(now, piece, 0)
        flying.sort(key=lambda f: f[:2])
        if unit < len(units) and (not flying or flying[0][0] > now):
            now += units[unit]
            unit += 1
            continue
        done, _, piece, step = flying.pop(0)
        now = max(now, done) + 0.4 + piece.traffic(step)[1] / 4e6
        events.append((unit, piece, step))
        if step + 1 < piece.steps:
            start(now, piece, step + 1)
    return events


def sum_scratch(pieces):
    out = []
    for piece in pieces:
        bufs = []
        for slabs, (stage, size, how) in zip(piece.slabs, piece.reduce):
            bufs.append(pltpu.VMEM((slabs, size, 256), BF))
        bufs += [pltpu.SemaphoreType.DMA((piece.steps,)), pltpu.SemaphoreType.DMA((piece.steps,)), pltpu.SemaphoreType.DMA((3,)), pltpu.SemaphoreType.REGULAR]
        out.append(bufs)
    return out


def add_rows(target, source, start, count):
    step = next(s for s in (192, 144, 96, 48, 16) if count % s == 0)

    def one(rows):
        offset = rows.start
        target[rows, :] = target[rows, :] + source[pl.ds(pl.multiple_of(start + offset, 16), step), :]

    by_rows(count, step, one)


class Exchange:
    def __init__(self, stages, source, gathered, outs, norm_all, norm_recv, norm_sems, table):
        self.source, self.gathered, self.outs = source, gathered, outs
        self.norm_all, self.norm_recv, self.norm_sems = norm_all, norm_recv, norm_sems
        self.table = table
        self.stages = stages
        self.place = Place(stages)
        self.regions = {}
        for piece in table:
            start, self.regions[piece] = piece.first, [piece.first]
            for stage, size, how in piece.reduce:
                if how == "half":
                    start = start + self.place.bits[stage] * size
                self.regions[piece].append(start)

    def barrier(self):
        sem = pltpu.get_barrier_semaphore()
        for stage in self.stages:
            pl.semaphore_signal(sem, inc=1, device_id=self.place.partners[stage], device_id_type=MESH)
        pl.semaphore_wait(sem, len(self.stages))

    def refs(self, piece):
        bufs = self.table[piece]
        n = len(piece.reduce)
        return bufs[:n], bufs[n], bufs[n + 1], bufs[n + 2], bufs[n + 3]

    def rows(self, start, size):
        return pl.ds(pl.multiple_of(start, 16), size)

    def region(self, piece, after):
        return self.regions[piece][after]

    def copy(self, piece, step):
        if piece.kind == "N":
            return pltpu.make_async_remote_copy(
                src_ref=self.norm_all.at[step], dst_ref=self.norm_recv.at[step],
                send_sem=self.norm_sems.at[0, step], recv_sem=self.norm_sems.at[1, step],
                device_id=self.place.partners[piece.order[step]], device_id_type=MESH,
            )
        recv, send_sem, recv_sem, _, _ = self.refs(piece)
        n = len(piece.reduce)
        if step < n:
            stage, size, how = piece.reduce[step]
            other = 1 - self.place.bits[stage]
            if step == 0:
                rows = self.rows(piece.first + other * size, size)
                src = self.source.at[:, rows, :] if piece.kind == "F" else self.gathered["A"].at[rows, :]
            elif how == "slab":
                src = recv[step - 1].at[1]
            elif how == "whole":
                src = recv[step - 1]
            else:
                src = recv[step - 1].at[:, self.rows(other * size, size), :]
            dst = recv[step].at[0] if how == "slab" or (step == 0 and piece.kind == "A") else recv[step]
        else:
            stage, size = piece.gather[step - n]
            count = next(i for i, r in enumerate(piece.reduce) if r[0] == stage)
            rows = self.rows(self.region(piece, count + 1), size)
            src = dst = self.gathered[piece.kind].at[rows, :]
        return pltpu.make_async_remote_copy(
            src_ref=src, dst_ref=dst, send_sem=send_sem.at[step], recv_sem=recv_sem.at[step],
            device_id=self.place.partners[stage], device_id_type=MESH,
        )

    def own_copies(self, piece):
        stage, size, _ = piece.reduce[0]
        rows = self.rows(piece.first + self.place.bits[stage] * size, size)
        return [
            pltpu.make_async_copy(
                self.source.at[i, rows, :],
                self.gathered["F"].at[pl.ds(piece.first + i * size, size), :],
                self.refs(piece)[3].at[i],
            )
            for i in range(2)
        ]

    def out_copy(self, piece):
        rows = pl.ds(piece.first, piece.rows)
        return pltpu.make_async_copy(
            self.gathered[piece.kind].at[rows, :], self.outs[piece.kind].at[rows, :], self.refs(piece)[3].at[2]
        )

    def begin(self, piece):
        self.copy(piece, 0).start()

    def arrive(self, piece, step):
        if step < 0:
            self.begin(piece)
            return
        self.copy(piece, step).wait_recv()
        if piece.kind == "N":
            self.norm_all[step + 1] = self.norm_all[step] + self.norm_recv[step]
            if step + 1 < piece.steps:
                self.copy(piece, step + 1).start()
            return
        recv = self.refs(piece)[0]
        all_rows = self.gathered[piece.kind]
        n = len(piece.reduce)
        more = step + 1 < piece.steps
        if step < n:
            stage, size, how = piece.reduce[step]
            if step == 0 and piece.kind == "F":
                for copy in self.own_copies(piece):
                    copy.wait()
            for slab in range(piece.slabs[step]):
                if step == 0:
                    start = piece.first + slab * size if piece.kind == "F" else piece.first + self.place.bits[stage] * size
                    add_rows(recv[0].at[slab], all_rows, start, size)
                else:
                    start = self.place.bits[stage] * size if how == "half" else 0
                    add_rows(recv[step].at[slab], recv[step - 1].at[slab], start, size)
            if step == 0:
                if piece.kind == "A":
                    self.copy(piece, 0).wait_send()
                pl.semaphore_signal(
                    self.refs(piece)[4], inc=1, device_id=self.place.partners[stage], device_id_type=MESH
                )
            if step == n - 1:
                all_rows[self.rows(self.region(piece, n), piece.size), :] = recv[step][0]
        if more:
            if step + 1 >= n and piece.gather[step + 1 - n][0] == piece.reduce[0][0]:
                pl.semaphore_wait(self.refs(piece)[4], 1)
            self.copy(piece, step + 1).start()
        if step + 1 == piece.steps:
            self.out_copy(piece).start()

    def end(self, pieces):
        for piece in pieces:
            for step in range(1 if piece.kind == "A" else 0, piece.steps):
                self.copy(piece, step).wait_send()
            if piece.kind != "N":
                self.out_copy(piece).wait()


FORWARD_CHUNK = 256
SLOTS = 2


def lines_of(j):
    return slice(256 * j, 256 * (j + 1))


CHUNK = 256


def sums_kernel(
    unit_rows, pieces, norms, events,
    grad_f, grad_long, norm_two, norm_long, n_hbm, middle_hbm, up_a, up_b, down_a, down_b,
    x_hbm, mg_hbm, u_hbm, v_hbm, phi_hbm, att_hbm, under_hbm, low_hbm, state_hbm,
    lengths, gain_ref, wq_h, wk_h, wv_h, wo_h, cos_ref, sin_ref, proj_ref, mask_ref,
    out_f, out_a, norm_out, mixed_hbm, ig_ref,
    all_f, all_a, norm_all, norm_recv, norm_sems, n_s, middle_s, mixed_s, wide, downs,
    x_s, mg_s, qk_s, ga_s, phi_s, v_s, attf_s, state_s, bw_s, load_sems, unit_sems, state_sems, *buffers,
):
    table, at = {}, 0
    for piece in pieces:
        if piece.kind != "N":
            count = 4 + len(piece.reduce)
            table[piece] = buffers[at : at + count]
            at += count
    work = Exchange(
        norms.order, grad_f, {"F": all_f, "A": all_a}, {"F": out_f, "A": out_a}, norm_all, norm_recv, norm_sems, table
    )
    tiles = n_hbm.shape[0] // unit_rows
    mols, size, width = x_s.shape
    slots = mols * size
    features = proj_ref.shape[1]
    lanes, deep = GROUP * HD, GROUP * features
    groups = H // GROUP
    half = up_a.shape[1]
    grads_s = [wide.at[pl.ds(i * slots, slots), :] for i in range(4)]
    low_s, att_s = (wide.at[pl.ds(i * slots, slots), :] for i in (4, 5))

    def weight(i):
        return downs.at[i // 2, pl.ds(i % 2 * width, width), :]

    copies = lambda pairs, first: [
        pltpu.make_async_copy(source, target, load_sems.at[first + i]) for i, (source, target) in enumerate(pairs)
    ]
    attention_loads = copies(
        [(w, weight(i)) for i, w in enumerate((wq_h, wk_h, wv_h, wo_h))]
        + [
            (x_hbm.at[:, pl.ds(0, size), :], x_s), (mg_hbm, mg_s), (u_hbm, qk_s), (v_hbm, v_s),
            (phi_hbm, phi_s), (att_hbm, attf_s), (under_hbm, ga_s), (low_hbm, low_s),
        ],
        9 + 2 * half // width,
    )

    def state_load(i):
        slot = lax.rem(i, 2)
        return pltpu.make_async_copy(state_hbm.at[pl.ds(2 * i, 2)], state_s.at[slot], state_sems.at[slot])

    blocks = half // width
    up_loads = copies(
        [
            (up.at[:, pl.ds(j * width, width)], wide.at[pl.ds((part * blocks + j) * width, width), :])
            for part, up in enumerate((up_a, up_b))
            for j in range(blocks)
        ],
        9,
    )
    down_loads = copies([(down_a, downs.at[0]), (down_b, downs.at[1])], 6)
    long_load = copies([(grad_long, all_a)], 8)

    def tile_loads(i):
        slot = lax.rem(i, SLOTS)
        rows = pl.ds(pl.multiple_of(i * unit_rows, 16), unit_rows)
        return (
            pltpu.make_async_copy(n_hbm.at[rows, :], n_s.at[slot], unit_sems.at[0, slot]),
            pltpu.make_async_copy(middle_hbm.at[rows, :], middle_s.at[slot], unit_sems.at[1, slot]),
        )

    def tile_store(i):
        slot = lax.rem(i, 2)
        rows = pl.ds(pl.multiple_of(i * unit_rows, 16), unit_rows)
        return pltpu.make_async_copy(mixed_s.at[slot], mixed_hbm.at[rows, :], unit_sems.at[2, slot])

    def project(i):
        for copy in attention_loads:
            copy.wait()
        build_features(proj_ref, None, bw_s)
        for k in range(slots // CHUNK):
            rows = slice(k * CHUNK, (k + 1) * CHUNK)
            place = lax.broadcasted_iota(jnp.int32, (size, width), 0)
            inside = []
            for b in range(k * CHUNK // size, (k + 1) * CHUNK // size):
                real = jnp.where(lengths[b] <= SHORT, lengths[b], 0)
                inside.append(jnp.where(place < real, mg_s[b * size : (b + 1) * size, :], 0.0))
            middle_grad = jnp.concatenate(inside, 0)
            mg_s[rows, :] = middle_grad
            branch = middle_grad.astype(BF)
            grads_s[3][rows, :] = branch
            att_s[rows, :] = attf_s[rows, :].astype(BF)
            ga_s[rows, :] = ga_s[rows, :] * nt(branch, weight(3)[...])

    def repeated(ref):
        return jnp.concatenate([ref[:size, :]] * (CHUNK // size), 0)

    def pair(i):
        mask = mask_ref[...]

        state_load(i).wait()
        slot = lax.rem(i, 2)
        places = [
            (
                pl.ds(pl.multiple_of((2 * i + m) * size, size), size),
                slice(g * lanes, (g + 1) * lanes),
                slice(g * deep, (g + 1) * deep),
            )
            for m in range(2)
            for g in range(groups)
        ]
        phis = [(phi_s[0, rows, spot], phi_s[1, rows, spot]) for rows, _, spot in places]
        items = [
            (phi_q.astype(BF), phi_k.astype(BF), with_ones(v_s[rows, cols]))
            for (phi_q, phi_k), (rows, cols, _) in zip(phis, places)
        ]
        overs = [ga_s[rows, cols] for rows, cols, _ in places]
        results = [
            (attf_s[rows, cols], None, state_s[slot, k // groups, k % groups])
            for k, (rows, cols, _) in enumerate(places)
        ]
        backs = attend_back(items, results, overs, mask)
        for (rows, cols, spot), (phi_q, phi_k), (dphi_q, dphi_k, dv) in zip(places, phis, backs):
            grads_s[2][rows, cols] = dv.astype(BF)
            phi_s[0, rows, spot] = dphi_q * phi_q
            phi_s[1, rows, spot] = dphi_k * phi_k

        @pl.when(i + 2 < mols // 2)
        def _():
            state_load(i + 2).start()

    def lower(i):
        rows = pl.ds(pl.multiple_of(i * CHUNK, CHUNK), CHUNK)
        cos, sin = repeated(cos_ref), repeated(sin_ref)
        for g in range(groups):
            cols = slice(g * lanes, (g + 1) * lanes)
            places = slice(g * deep, (g + 1) * deep)
            u = jnp.concatenate([qk_s[0, rows, cols], qk_s[1, rows, cols]], 0)
            du = pull_features(jnp.concatenate([phi_s[0, rows, places], phi_s[1, rows, places]], 0), u, bw_s[g])
            grads_s[0][rows, cols] = rotate(du[:CHUNK], cos, -sin).astype(BF)
            grads_s[1][rows, cols] = rotate(du[CHUNK:], cos, -sin).astype(BF)

    def inputs(i):
        gain = line(gain_ref)
        rows_sum = [norm_long[0:1, :], norm_long[1:2, :]]
        for k in range(slots // CHUNK):
            rows = slice(k * CHUNK, (k + 1) * CHUNK)
            parts = slice(k * CHUNK // size, (k + 1) * CHUNK // size)
            grad = nt(grads_s[0][rows, :], weight(0)[...])
            grad = grad + nt(grads_s[1][rows, :], weight(1)[...])
            grad = grad + nt(grads_s[2][rows, :], weight(2)[...])
            n, scale = norm_parts(x_s[parts].reshape(CHUNK, width).astype(F32))
            e = grad * gain
            mean_e = jnp.mean(e, -1, keepdims=True)
            mean_en = jnp.mean(e * n, -1, keepdims=True)
            out = mg_s[rows, :] + scale * (e - mean_e - n * mean_en)
            ig_ref[parts] = out.astype(BF).reshape(CHUNK // size, size, width)
            rows_sum[0] = rows_sum[0] + jnp.sum(grad * n, 0, keepdims=True)
            rows_sum[1] = rows_sum[1] + jnp.sum(grad, 0, keepdims=True)
        norm_all[0] = jnp.concatenate(rows_sum + [norm_two[0:2, :], jnp.zeros((4, width), F32)], 0)
        for copy in up_loads + down_loads:
            copy.start()

    def product(part):
        if part == 0:
            long_load[0].wait()
        left = att_s if part == 0 else low_s
        right = grads_s[(3, 2, 0, 1)[part]]
        for r in range(width // 256):
            grad = tn(left[:, lines_of(r)], right[...])
            for j in range(width // 256):
                base = (part * (width // 256) + j) * width + 256 * r
                rows = slice(base, base + 256)
                all_a[rows, :] = (all_a[rows, :].astype(F32) + grad[:, lines_of(j)]).astype(BF)

    def forward(i):
        slot = lax.rem(i, SLOTS)

        @pl.when(i == 0)
        def _():
            for copy in up_loads + down_loads:
                copy.wait()

        @pl.when(i + SLOTS - 1 < tiles)
        def _():
            for copy in tile_loads(i + SLOTS - 1):
                copy.start()

        for copy in tile_loads(i):
            copy.wait()
        n = n_s[slot]
        for part in range(2):
            total = middle_s[slot]
            chunks = range(part * half // FORWARD_CHUNK, (part + 1) * half // FORWARD_CHUNK)

            def enter(k):
                block, lane = k * FORWARD_CHUNK // width, k * FORWARD_CHUNK % width
                return nn(n, wide[block * width : (block + 1) * width, lane : lane + FORWARD_CHUNK])

            ahead = enter(chunks[0])
            for k in chunks:
                h = ahead
                if k + 1 in chunks:
                    ahead = enter(k + 1)
                place = k * FORWARD_CHUNK % half
                total = total + nn(gelu(h), downs[part, place : place + FORWARD_CHUNK, :])
            if part == 0:
                middle_s[slot] = total
                between(i)

        @pl.when(i >= 2)
        def _():
            tile_store(i - 2).wait()

        mixed_s[lax.rem(i, 2)] = total.astype(BF)
        tile_store(i).start()

    def happen(unit):
        for when, piece, step in events:
            if when == unit:
                work.arrive(piece, step)

    def between(i):
        for k in range(tiles):
            at = forward_unit + 2 * k + 1
            if any(when == at for when, _, _ in events):
                pl.when(i == k)(functools.partial(happen, at))

    for copy in attention_loads + [state_load(0), state_load(1)] + long_load:
        copy.start()
    for i in range(min(SLOTS - 1, tiles)):
        for copy in tile_loads(i):
            copy.start()
    for piece in pieces:
        if piece.kind == "F":
            for copy in work.own_copies(piece):
                copy.start()
    work.barrier()
    happen(0)
    unit = 0
    kinds = unit_list(slots, mols, tiles, project, pair, lower, inputs, product, forward)
    forward_unit = sum(count for count, _ in kinds[:-1])
    for count, run in kinds:
        stride = 2 if run is forward else 1
        if count == 1:
            run(0)
            happen(unit + 1)
        else:

            def body(i, carry, unit=unit, run=run, count=count, stride=stride):
                run(i)
                for k in range(count):
                    at = unit + (k + 1) * stride
                    if any(when == at for when, _, _ in events):
                        pl.when(i == k)(functools.partial(happen, at))
                return carry

            lax.fori_loop(0, count, body, 0)
        unit += count
    norm_out[...] = norm_all[norms.steps]
    for i in range(max(tiles - 2, 0), tiles):
        tile_store(i).wait()
    work.end(pieces)


def unit_list(slots, mols, tiles, project, pair, lower, inputs, product, forward):
    chunks = slots // CHUNK
    one = [(1, lambda i, part=part: product(part)) for part in range(4)]
    return [
        (1, project), one[0], (mols // 2, pair), one[1], (chunks, lower), one[2], one[3], (1, inputs), (tiles, forward),
    ]


PRODUCT_KINDS = (1, 3, 5, 6)
UNIT_US = (3.5, 1.5, 3.0, 1.5, 2.0, 1.5, 1.5, 3.0, 1.6)


def sums(
    dp, grad_f, grad_long, norm_two, norm_long, normed, middle, ups, downs, tokens, mg, saved, lengths, gain, weights,
    tables, projection, mask,
):
    mols, seq, width = tokens.shape
    rows = mols * seq
    half = ups[0].shape[1]
    slots = mols * SHORT
    tiles = mols
    block_rows, att_rows = grad_f.shape[1], grad_long.shape[0]
    heads, features, size = projection.shape
    groups = heads // GROUP
    f_pieces, a_pieces, norms = pieces_of(dp, block_rows, att_rows)
    costs, after = [], []
    for (count, _), cost in zip(unit_list(slots, mols, tiles, *[None] * 6), UNIT_US):
        costs += [cost] * count
        after.append(len(costs))
    costs += [costs[-1]] * tiles
    ready = {piece: 0 for piece in f_pieces}
    ready[norms] = after[-2]
    for piece in a_pieces:
        part = (piece.first + piece.rows - 1) // (width * (width // 256))
        ready[piece] = after[PRODUCT_KINDS[part]]
    pieces = f_pieces + a_pieces + [norms]
    events = schedule(pieces, ready, costs)
    u, v, phi, att, under, low, state = saved
    hbm = pl.BlockSpec(memory_space=pl.ANY)
    vmem = pl.BlockSpec(memory_space=pltpu.VMEM)
    return pl.pallas_call(
        functools.partial(sums_kernel, seq, pieces, norms, events),
        in_specs=[hbm, hbm, vmem, vmem] + [hbm] * 15 + [pl.BlockSpec(memory_space=pltpu.SMEM), vmem] + [hbm] * 4 + [vmem] * 4,
        out_specs=[hbm, hbm, vmem, hbm, vmem],
        out_shape=[
            jax.ShapeDtypeStruct((block_rows, 256), BF),
            jax.ShapeDtypeStruct((att_rows, 256), BF),
            jax.ShapeDtypeStruct(norm_two.shape, F32),
            jax.ShapeDtypeStruct((rows, width), BF),
            jax.ShapeDtypeStruct((mols, SHORT, width), BF),
        ],
        scratch_shapes=[
            pltpu.VMEM((block_rows, 256), BF),
            pltpu.VMEM((att_rows, 256), BF),
            pltpu.VMEM((norms.steps + 1,) + norm_two.shape, F32),
            pltpu.VMEM((norms.steps,) + norm_two.shape, F32),
            pltpu.SemaphoreType.DMA((2, norms.steps)),
            pltpu.VMEM((SLOTS, seq, width), BF),
            pltpu.VMEM((SLOTS, seq, width), F32),
            pltpu.VMEM((2, seq, width), BF),
            pltpu.VMEM((max(2 * half, 6 * slots), width), BF),
            pltpu.VMEM((2, half, width), BF),
            pltpu.VMEM((mols, SHORT, width), BF),
            pltpu.VMEM((slots, width), F32),
            pltpu.VMEM((2, slots, width), F32),
            pltpu.VMEM((slots, width), F32),
            pltpu.VMEM((2, slots, heads * features), F32),
            pltpu.VMEM((slots, width), BF),
            pltpu.VMEM((slots, width), F32),
            pltpu.VMEM((2, 2) + saved[-1].shape[1:], BF),
            pltpu.VMEM((groups, 3 * GROUP * features, 2 * GROUP * size), BF),
            pltpu.SemaphoreType.DMA((9 + 2 * half // width + 12,)),
            pltpu.SemaphoreType.DMA((3, SLOTS)),
            pltpu.SemaphoreType.DMA((2,)),
        ]
        + [b for bufs in sum_scratch(f_pieces + a_pieces) for b in bufs],
        compiler_params=pltpu.CompilerParams(
            vmem_limit_bytes=60 * 1024 * 1024, collective_id=0, has_side_effects=True
        ),
        name="gradient_sums",
    )(
        grad_f, grad_long, norm_two, norm_long, normed, middle, *ups, *downs, tokens, mg, u.reshape(2, slots, width), v.reshape(slots, width),
        phi.reshape(2, slots, -1), att.reshape(slots, width), under.reshape(slots, width), low.reshape(slots, width), state,
        lengths, gain, *weights, *tables, projection, mask,
    )


def widen_kernel(
    up_blocks, down_blocks, att_blocks, norms, mixed, ig_long, ig_short, up_ref, down_ref, q_ref, k_ref, v_ref, o_ref,
    norm_a, norm_b, norm_c, norm_d, mixed_out, ig_out,
):
    mixed_out[...] = mixed[...]
    size = ig_short.shape[1]
    ig_out[:, :size, :] = ig_long[:, :size, :] + ig_short[...]
    ig_out[:, size:, :] = ig_long[:, size:, :]

    @pl.when(pl.program_id(0) == 0)
    def _():
        for i, ref in enumerate((norm_a, norm_b, norm_c, norm_d)):
            ref[...] = norms[i, :]

    for j in range(up_blocks.shape[0]):
        up_ref[:, lines_of(j)] = up_blocks[j].astype(F32)
    for j in range(down_blocks.shape[0]):
        down_ref[:, lines_of(j)] = down_blocks[j].astype(F32)
    for i, ref in enumerate((o_ref, v_ref, q_ref, k_ref)):
        for j in range(att_blocks.shape[1]):
            ref[:, lines_of(j)] = att_blocks[i, j].astype(F32)


def widen(grad_f, grad_a, norms, mixed, ig_long, ig_short, width, half):
    blocks, ups = width // 256, half // 256
    mols, seq, _ = ig_long.shape
    cuts = mols
    rows = mixed.shape[0]
    att = jax.ShapeDtypeStruct((width, width), F32)
    att_spec = pl.BlockSpec((width // cuts, width), lambda r: (r, 0))
    vector = jax.ShapeDtypeStruct((width,), F32)
    vector_spec = pl.BlockSpec((width,), lambda r: (0,))
    ig_spec = lambda size: pl.BlockSpec((mols // cuts, size, width), lambda r: (r, 0, 0))
    mixed_spec = pl.BlockSpec((rows // cuts, width), lambda r: (r, 0))
    return pl.pallas_call(
        widen_kernel,
        grid=(cuts,),
        in_specs=[
            pl.BlockSpec((ups, width // cuts, 256), lambda r: (0, r, 0)),
            pl.BlockSpec((blocks, half // cuts, 256), lambda r: (ups * width // (half * blocks), r, 0)),
            pl.BlockSpec((4, blocks, width // cuts, 256), lambda r: (0, 0, r, 0)),
            pl.BlockSpec(norms.shape, lambda r: (0, 0)),
            mixed_spec, ig_spec(seq), ig_spec(ig_short.shape[1]),
        ],
        out_specs=[
            pl.BlockSpec((width // cuts, half), lambda r: (r, 0)),
            pl.BlockSpec((half // cuts, width), lambda r: (r, 0)),
            att_spec, att_spec, att_spec, att_spec,
            vector_spec, vector_spec, vector_spec, vector_spec, mixed_spec, ig_spec(seq),
        ],
        out_shape=[
            jax.ShapeDtypeStruct((width, half), F32),
            jax.ShapeDtypeStruct((half, width), F32),
            att, att, att, att, vector, vector, vector, vector,
            jax.ShapeDtypeStruct(mixed.shape, BF),
            jax.ShapeDtypeStruct(ig_long.shape, BF),
        ],
        compiler_params=pltpu.CompilerParams(vmem_limit_bytes=VMEM_LIMIT),
        name="widen",
    )(
        grad_f.reshape(-1, width, 256), grad_f.reshape(-1, half, 256),
        grad_a.reshape(4, blocks, width, 256), norms, mixed, ig_long, ig_short,
    )


def local(
    dp, tokens, gain_one, shift_one, query_weight, key_weight, value_weight, out_weight, gain_two, shift_two,
    up_weight, down_weight, lengths, projection, cotangent,
):
    mols, seq, width = tokens.shape
    rows = mols * seq
    half = up_weight.shape[1]
    features = projection.shape[2]
    mask = jnp.asarray(np.tile(head_mask(features), (1, 2)))
    tables = tuple(jnp.asarray(t) for t in rotary_tables(seq))
    weights = (query_weight, key_weight, value_weight, out_weight)
    projection = jnp.swapaxes(projection, 1, 2)
    middle, normed, up_other, down_other, *saved = attention_forward(
        tokens, lengths, gain_one, shift_one, *weights, gain_two, shift_two, tables, projection, mask,
        up_weight, down_weight,
    )
    grad_ffn, mg_long, mg_short, norm_two = ffn_backward(
        normed, cotangent.reshape(rows, width), middle, up_weight, up_other, down_weight, down_other,
        gain_two, lengths, seq,
    )
    ig_long, grad_long, norm_long = long_backward(
        tokens, mg_long, lengths, gain_one, shift_one, *weights, tables, projection, mask
    )
    sum_f, sum_a, norms, mixed, ig_short = sums(
        dp, grad_ffn, grad_long, norm_two, norm_long, normed, middle, (up_weight, up_other), (down_weight, down_other),
        tokens, mg_short, saved, lengths, gain_one, weights, tables, projection, mask,
    )
    up_grad, down_grad, q, k, v, o, g1, s1, g2, s2, mixed, input_grad = widen(
        sum_f, sum_a, norms, mixed, ig_long, ig_short, width, half
    )
    return (mixed.reshape(tokens.shape), input_grad, g1, s1, q, k, v, o, g2, s2, up_grad, down_grad)


def solution(mesh):
    placed = (
        P(("dp", "ffn"), None, None), P(), P(), P(), P(), P(), P(), P(), P(), P(None, "ffn"), P("ffn", None),
        P(("dp", "ffn")), P(), P(("dp", "ffn"), None, None),
    )
    return jax.shard_map(
        functools.partial(local, mesh.shape["dp"]),
        mesh=mesh,
        in_specs=placed,
        out_specs=(
            P(("dp", "ffn"), None, None), P(("dp", "ffn"), None, None), P(), P(), P(), P(), P(), P(), P(), P(),
            P(None, "ffn"), P("ffn", None),
        ),
        check_vma=False,
    )
```
